32 devices in a mesh: tm: 8 (over z, y), row: 4 (over x, core).
Axes of the slice: x: 2, y: 2, z: 4, core: 2. Of those that a mesh axis runs over, the one named last changes fastest.
Arguments:
- precisions: float32 [8, 1024, 1024], P('tm', 'row'), as said below
- couplings: float32 [8, 1024, 1024], P('tm', 'row'), as said below
- right_sides: float32 [8, 1024, 256], P('tm', 'row'), may hold values from -6 to 6
Outputs:
- pivot_blocks: float32 [8, 1024, 1024], P('tm', 'row')
- coupling_blocks: float32 [8, 1024, 1024], P('tm', 'row')
- reduced_sides: float32 [8, 1024, 256], P('tm', 'row')
The draws below stay inside these ranges and needn't reach their ends.
Inputs may be any that keep to these rules, and one draw needn't show every extreme that they name: precisions and couplings together form a symmetric positive definite block-tridiagonal matrix whose eigenvalues are 1 or more; couplings[0] is zero. `couplings`: see precisions.
All inputs are finite; a program needn't handle non-finite values.
Results may differ from the reference program's by a relative error of at most 0.00023.
Values sent between devices are 32-bit elements; how exact they have to be, the bound alone decides.
A program may use at most 128 MiB of HBM per device.

```python
import math
import jax
import jax.numpy as jnp
from jax import lax

D = 1024
RHS_COLS = 256
LEVELS = 2
BLOCKS = 8


def lag_factors(base_key):
    seeded = jax.random.fold_in(base_key, 11)
    gain_key, diag_key, lag_key = jax.random.split(seeded, 3)
    scale = 0.5 / math.sqrt(D)
    gains = jax.random.uniform(gain_key, (BLOCKS, D), jnp.float32, 1.0, 2.0)
    diag_noise = jax.random.normal(diag_key, (BLOCKS, D, D), jnp.float32)
    lag_noise = jax.random.normal(lag_key, (BLOCKS, D, D), jnp.float32)
    identity = jnp.eye(D, dtype=jnp.float32)
    diag_factor = gains[:, :, None] * identity[None, :, :] + scale * diag_noise
    later = (jnp.arange(BLOCKS) > 0).astype(jnp.float32)
    lag_factor = (0.9 * identity[None, :, :] + scale * lag_noise) * later[:, None, None]
    return (diag_factor, lag_factor)


def draw_precisions(key, part):
    diag_factor, lag_factor = lag_factors(key)
    exact = lax.Precision.HIGHEST
    own = jnp.einsum('tij,tkj->tik', diag_factor, diag_factor, precision=exact)
    lagged = jnp.einsum('tij,tkj->tik', lag_factor, lag_factor, precision=exact)
    identity = jnp.eye(D, dtype=jnp.float32)
    return own + lagged + identity[None, :, :]


def draw_couplings(key, part):
    diag_factor, lag_factor = lag_factors(key)
    earlier = jnp.roll(diag_factor, 1, axis=0)
    return jnp.einsum('tij,tkj->tik', earlier, lag_factor, precision=lax.Precision.HIGHEST)


def block_scale(key, dims, pieces, low, high):
    def one(position, shards_of):
        draws = jax.random.uniform(jax.random.fold_in(jax.random.fold_in(key, 6), position), (shards_of,), jnp.float32, low / len(pieces), high / len(pieces))
        return jnp.repeat(jnp.exp(draws), dims[position] // shards_of).reshape((-1,) + (1,) * (len(dims) - position - 1))

    factor_of = one(*pieces[0])
    for cut in pieces[1:]:
        factor_of = factor_of * one(*cut)
    return factor_of


def centred(stream_key, extent, deviation, reach, shards=(), kind=jnp.bfloat16):
    array = deviation * jax.random.normal(stream_key, extent, jnp.float32)
    if shards:
        array = array * block_scale(stream_key, extent, shards, -0.22, 0.18)
    return jnp.clip(array, -reach, reach).astype(kind)


def setup_inputs(seed: int = 0) -> dict:
    seeds = jax.random.split(jax.random.key(seed), 4)
    return {
        "precisions": draw_precisions(jax.random.fold_in(seeds[3], 71), 0),
        "couplings": draw_couplings(jax.random.fold_in(seeds[3], 71), 0),
        "right_sides": centred(seeds[2], (BLOCKS, D, RHS_COLS), 1.0, 6.0, ((0, 8), (1, 4)), jnp.float32),
    }


def product(left, right):
    return lax.dot_general(left, right, (((0,), (0,)), ((), ())), precision=lax.Precision.HIGHEST)

def reference(precisions, couplings, right_sides):
    block_count = precisions.shape[0]
    pivot_list = [precisions[block_index] for block_index in range(block_count)]
    coupling_list = [jnp.zeros_like(couplings[0])] + [couplings[block_index] for block_index in range(1, block_count)]
    side_list = [right_sides[block_index] for block_index in range(block_count)]
    for level_step in range(LEVELS):
        level_stride = 2 ** level_step
        new_pivots = list(pivot_list)
        new_couplings = list(coupling_list)
        new_sides = list(side_list)
        for middle in range(block_count):
            lower_fac = jnp.linalg.cholesky(pivot_list[middle])
            left_solve = jax.scipy.linalg.solve_triangular(lower_fac, coupling_list[middle].T, lower=True)
            side_solve = jax.scipy.linalg.solve_triangular(lower_fac, side_list[middle], lower=True)
            before = middle - level_stride
            if before >= 0:
                new_pivots[before] = new_pivots[before] - product(left_solve, left_solve)
                new_sides[before] = new_sides[before] - product(left_solve, side_solve)
            after_index = middle + level_stride
            if after_index < block_count:
                right_solve = jax.scipy.linalg.solve_triangular(lower_fac, coupling_list[after_index], lower=True)
                new_pivots[after_index] = new_pivots[after_index] - product(right_solve, right_solve)
                new_sides[after_index] = new_sides[after_index] - product(right_solve, side_solve)
                new_couplings[after_index] = -product(left_solve, right_solve)
        for early in range(min(level_stride, block_count)):
            new_couplings[early] = jnp.zeros_like(coupling_list[early])
        pivot_list = new_pivots
        coupling_list = new_couplings
        side_list = new_sides
    return (jnp.stack(pivot_list), jnp.stack(coupling_list), jnp.stack(side_list))
```

```python
import jax
import jax.numpy as jnp
from jax import lax
from jax.experimental import pallas as pl
from jax.experimental.pallas import tpu as pltpu
from jax.sharding import PartitionSpec as P

LEVELS = 2
BLOCK = 128
PANEL = 8


def split(x):
    high = x.astype(jnp.bfloat16)
    low = (x - high.astype(jnp.float32)).astype(jnp.bfloat16)
    return high, low


def dot(left, right):
    return lax.dot_general(
        left, right, (((1,), (0,)), ((), ())), preferred_element_type=jnp.float32
    )


def sweep_small(entry):
    for p in range(PANEL):
        scale = 1.0 / entry[p, p]
        old = {i: entry[min(i, p), max(i, p)] for i in range(PANEL) if i != p}
        new = {i: old[i] * scale for i in old}
        for i in old:
            for j in old:
                if i <= j:
                    entry[i, j] = entry[i, j] - new[i] * old[j]
        for i in old:
            entry[min(i, p), max(i, p)] = new[i]
        entry[p, p] = -scale
    return entry


def sweep_block(block):
    shape = (PANEL, BLOCK)
    lane = lax.broadcasted_iota(jnp.int32, shape, 1)
    sublane = lax.broadcasted_iota(jnp.int32, shape, 0)
    count = BLOCK // PANEL
    tiles = [block[PANEL * i:PANEL * (i + 1), :] for i in range(count)]
    for k in range(count):
        c = PANEL * k
        inside = (lane >= c) & (lane < c + PANEL)
        cols = [
            [jnp.broadcast_to(tiles[i][:, c + j:c + j + 1], shape) for j in range(PANEL)]
            for i in range(count)
        ]
        entry = {
            (i, j): jnp.broadcast_to(cols[k][j][i:i + 1, :], shape)
            for i in range(PANEL) for j in range(i, PANEL)
        }
        rows = [
            jnp.where(
                inside,
                jnp.where(lane == c + j, -1.0, 0.0),
                jnp.broadcast_to(tiles[k][j:j + 1, :], shape),
            )
            for j in range(PANEL)
        ]
        entry = sweep_small(entry)
        solved = []
        for i in range(PANEL):
            total = entry[min(i, 0), max(i, 0)] * rows[0]
            for j in range(1, PANEL):
                total = total + entry[min(i, j), max(i, j)] * rows[j]
            solved.append(-total)
        for i in range(count):
            if i == k:
                tile = solved[0]
                for j in range(1, PANEL):
                    tile = jnp.where(sublane == j, solved[j], tile)
            else:
                tile = jnp.where(inside, 0.0, tiles[i])
                for j in range(PANEL):
                    tile = tile - cols[i][j] * solved[j]
            tiles[i] = tile
    return jnp.concatenate(tiles, axis=0)


def inverse_kernel(a_ref, x_ref, left_ref, right_ref):
    order = a_ref.shape[0]
    count = order // BLOCK
    width = min(order, 256)
    x_ref[...] = a_ref[...]

    @pl.loop(0, count)
    def _(k):
        start = pl.multiple_of(k * BLOCK, BLOCK)
        mine = pl.ds(start, BLOCK)
        negative = sweep_block(x_ref[mine, mine])
        high, low = split(x_ref[:, mine])
        left_ref[:, 0:BLOCK] = high
        left_ref[:, BLOCK:2 * BLOCK] = high
        left_ref[:, 2 * BLOCK:3 * BLOCK] = low
        row = lax.broadcasted_iota(jnp.int32, (BLOCK, BLOCK), 0)
        col = lax.broadcasted_iota(jnp.int32, (BLOCK, BLOCK), 1)
        x_ref[mine, mine] = jnp.where(row == col, -1.0, 0.0)
        n_high, n_low = split(-negative)
        factor = jnp.concatenate([n_high, n_high, n_low], axis=1)
        p_high, p_low = split(x_ref[mine, :])
        solved = dot(factor, jnp.concatenate([p_high, p_low, p_high], axis=0))
        s_high, s_low = split(solved)
        right_ref[0:BLOCK, :] = s_high
        right_ref[BLOCK:2 * BLOCK, :] = s_low
        right_ref[2 * BLOCK:3 * BLOCK, :] = s_high
        x_ref[:, mine] = jnp.zeros((order, BLOCK), jnp.float32)

        @pl.loop(0, order // width)
        def _(n):
            cols = pl.ds(pl.multiple_of(n * width, width), width)
            x_ref[:, cols] = x_ref[:, cols] - dot(left_ref[...], right_ref[:, cols])

        x_ref[mine, :] = solved


def negative_inverse(matrix):
    order = matrix.shape[0]
    return pl.pallas_call(
        inverse_kernel,
        out_shape=jax.ShapeDtypeStruct((order, order), jnp.float32),
        in_specs=[pl.BlockSpec(memory_space=pltpu.VMEM)],
        out_specs=pl.BlockSpec(memory_space=pltpu.VMEM),
        scratch_shapes=[
            pltpu.VMEM((order, 3 * BLOCK), jnp.bfloat16),
            pltpu.VMEM((3 * BLOCK, order), jnp.bfloat16),
        ],
        compiler_params=pltpu.CompilerParams(vmem_limit_bytes=32 * 2 ** 20),
        cost_estimate=pl.CostEstimate(
            flops=64 * order ** 3, bytes_accessed=8 * order * order, transcendentals=0
        ),
        name="negative_inverse",
    )(matrix)


def from_behind(block, axis, distance):
    devices = range(lax.axis_size(axis))
    route = [(i - distance, i) for i in devices if i - distance in devices]
    return lax.ppermute(block, axis, route)


def multiply(left, right, dims):
    return lax.dot_general(left, right, (dims, ((), ())), precision=lax.Precision.HIGH)


def local(precisions, couplings, right_sides):
    pivot, link, side = precisions[0], couplings[0], right_sides[0]
    rows = pivot.shape[0]
    row_start = lax.axis_index("row") * rows
    link = jnp.where(lax.axis_index("tm") == 0, jnp.zeros_like(link), link)
    for level in range(LEVELS):
        h = 1 << level
        whole_pivot = lax.all_gather(pivot, "row", axis=0, tiled=True)
        whole_side = lax.all_gather(side, "row", axis=0, tiled=True)
        whole_link = lax.all_gather(link, "row", axis=0, tiled=True)
        next_link = lax.all_gather(from_behind(link, "tm", -h), "row", axis=0, tiled=True)
        negative = negative_inverse(whole_pivot)
        next_cols = lax.dynamic_slice_in_dim(next_link, row_start, rows, 1)
        left = multiply(link, negative, ((1,), (0,)))
        right = multiply(next_cols, negative, ((0,), (0,)))
        left_block = multiply(left, whole_link, ((1,), (1,)))
        right_block = multiply(right, next_link, ((1,), (0,)))
        left_side = multiply(left, whole_side, ((1,), (0,)))
        right_side = multiply(right, whole_side, ((1,), (0,)))
        new_link = multiply(left, next_link, ((1,), (0,)))
        pivot = pivot + from_behind(left_block, "tm", -h) + from_behind(right_block, "tm", h)
        side = side + from_behind(left_side, "tm", -h) + from_behind(right_side, "tm", h)
        link = from_behind(new_link, "tm", h)
    return pivot[None], link[None], side[None]


def solution(mesh):
    placed = (P("tm", "row", None), P("tm", "row", None), P("tm", "row", None))
    return jax.shard_map(
        local, mesh=mesh, in_specs=placed, out_specs=placed, check_vma=False
    )
```

```python
import functools

import jax
import jax.numpy as jnp
from jax import lax
from jax.experimental import pallas as pl
from jax.experimental.pallas import tpu as pltpu
from jax.sharding import PartitionSpec as P

LEVELS = 2
BLOCK = 128
PANEL = 8


def split(x):
    high = x.astype(jnp.bfloat16)
    low = (x - high.astype(jnp.float32)).astype(jnp.bfloat16)
    return high, low


def dot(left, right):
    return lax.dot_general(
        left, right, (((1,), (0,)), ((), ())), preferred_element_type=jnp.float32
    )


def sweep_small(entry):
    for p in range(PANEL):
        scale = 1.0 / entry[p, p]
        old = {i: entry[min(i, p), max(i, p)] for i in range(PANEL) if i != p}
        new = {i: old[i] * scale for i in old}
        for i in old:
            for j in old:
                if i <= j:
                    entry[i, j] = entry[i, j] - new[i] * old[j]
        for i in old:
            entry[min(i, p), max(i, p)] = new[i]
        entry[p, p] = -scale
    return entry


def sweep_block(block, between=lambda k: None):
    shape = (PANEL, BLOCK)
    lane = lax.broadcasted_iota(jnp.int32, shape, 1)
    sublane = lax.broadcasted_iota(jnp.int32, shape, 0)
    count = BLOCK // PANEL
    tiles = [block[PANEL * i:PANEL * (i + 1), :] for i in range(count)]
    for k in range(count):
        c = PANEL * k
        inside = (lane >= c) & (lane < c + PANEL)
        cols = [
            [jnp.broadcast_to(tiles[i][:, c + j:c + j + 1], shape) for j in range(PANEL)]
            for i in range(count)
        ]
        entry = {
            (i, j): jnp.broadcast_to(cols[k][j][i:i + 1, :], shape)
            for i in range(PANEL) for j in range(i, PANEL)
        }
        rows = [
            jnp.where(
                inside,
                jnp.where(lane == c + j, -1.0, 0.0),
                jnp.broadcast_to(tiles[k][j:j + 1, :], shape),
            )
            for j in range(PANEL)
        ]
        entry = sweep_small(entry)
        solved = []
        for i in range(PANEL):
            total = entry[min(i, 0), max(i, 0)] * rows[0]
            for j in range(1, PANEL):
                total = total + entry[min(i, j), max(i, j)] * rows[j]
            solved.append(-total)
        for i in range(count):
            if i == k:
                tile = solved[0]
                for j in range(1, PANEL):
                    tile = jnp.where(sublane == j, solved[j], tile)
            else:
                tile = jnp.where(inside, 0.0, tiles[i])
                for j in range(PANEL):
                    tile = tile - cols[i][j] * solved[j]
            tiles[i] = tile
        between(k)
    return jnp.concatenate(tiles, axis=0)


def inverse_kernel(count, *refs):
    places, pieces = refs[0], refs[1:1 + count]
    x_ref, left_ref, right_ref, negative_ref = refs[1 + count:]
    order = x_ref.shape[0]
    rows = order // count
    steps = order // BLOCK
    size = min(order, 256)
    panels = BLOCK // PANEL
    chunks = [(m, n) for n in range(0, order, size) for m in range(0, order, size)]
    for place, piece in enumerate(pieces):
        x_ref[pl.ds(pl.multiple_of(places[place] * rows, rows), rows), :] = piece[...]

    def prepare(start):
        mine = pl.ds(start, BLOCK)
        high, low = split(x_ref[:, mine])
        left_ref[:, 0:BLOCK] = high
        left_ref[:, BLOCK:2 * BLOCK] = high
        left_ref[:, 2 * BLOCK:3 * BLOCK] = low
        row = lax.broadcasted_iota(jnp.int32, (BLOCK, BLOCK), 0)
        col = lax.broadcasted_iota(jnp.int32, (BLOCK, BLOCK), 1)
        x_ref[mine, mine] = jnp.where(row == col, -1.0, 0.0)
        n_high, n_low = split(-negative_ref[...])
        factor = jnp.concatenate([n_high, n_high, n_low], axis=1)
        p_high, p_low = split(x_ref[mine, :])
        solved = dot(factor, jnp.concatenate([p_high, p_low, p_high], axis=0))
        s_high, s_low = split(solved)
        right_ref[0:BLOCK, :] = s_high
        right_ref[BLOCK:2 * BLOCK, :] = s_low
        right_ref[2 * BLOCK:3 * BLOCK, :] = s_high
        x_ref[:, mine] = jnp.zeros((order, BLOCK), jnp.float32)
        return solved

    def update(m, n):
        x_ref[m:m + size, n:n + size] = x_ref[m:m + size, n:n + size] - dot(
            left_ref[m:m + size, :], right_ref[:, n:n + size]
        )

    negative_ref[...] = sweep_block(x_ref[0:BLOCK, 0:BLOCK])

    @pl.loop(0, steps - 1)
    def _(k):
        start = pl.multiple_of(k * BLOCK, BLOCK)
        solved = prepare(start)
        after = pl.ds(pl.multiple_of(start + BLOCK, BLOCK), BLOCK)
        following = x_ref[after, after] - dot(left_ref[after, :], right_ref[:, after])

        def between(panel):
            for chunk in chunks[panel * len(chunks) // panels:(panel + 1) * len(chunks) // panels]:
                update(*chunk)

        negative_ref[...] = sweep_block(following, between)
        x_ref[pl.ds(start, BLOCK), :] = solved

    last = order - BLOCK
    solved = prepare(last)
    for chunk in chunks:
        update(*chunk)
    x_ref[last:order, :] = solved


def negative_inverse(places, pieces):
    count = len(pieces)
    order = pieces[0].shape[1]
    return pl.pallas_call(
        functools.partial(inverse_kernel, count),
        out_shape=jax.ShapeDtypeStruct((order, order), jnp.float32),
        in_specs=[pl.BlockSpec(memory_space=pltpu.SMEM)]
        + [pl.BlockSpec(memory_space=pltpu.VMEM)] * count,
        out_specs=pl.BlockSpec(memory_space=pltpu.VMEM),
        scratch_shapes=[
            pltpu.VMEM((order, 3 * BLOCK), jnp.bfloat16),
            pltpu.VMEM((3 * BLOCK, order), jnp.bfloat16),
            pltpu.VMEM((BLOCK, BLOCK), jnp.float32),
        ],
        compiler_params=pltpu.CompilerParams(vmem_limit_bytes=32 * 2 ** 20),
        cost_estimate=pl.CostEstimate(
            flops=64 * order ** 3, bytes_accessed=8 * order * order, transcendentals=0
        ),
        name="negative_inverse",
    )(places, *pieces)


def swapped(block, axis, distance):
    return lax.ppermute(block, axis, [(i, i ^ distance) for i in range(lax.axis_size(axis))])


def gather_pieces(block):
    count = lax.axis_size("row")
    pieces = {0: block}
    for k in range(2, count, 2):
        pieces[k] = swapped(block, "row", k)
    for k in range(0, count, 2):
        pieces[k + 1] = swapped(pieces[k], "row", 1)
    return [pieces[k] for k in range(count)]


def from_behind(block, axis, distance):
    devices = range(lax.axis_size(axis))
    route = [(i - distance, i) for i in devices if i - distance in devices]
    return lax.ppermute(block, axis, route)


def multiply(left, right, dims):
    return lax.dot_general(left, right, (dims, ((), ())), precision=lax.Precision.HIGH)


def local(precisions, couplings, right_sides):
    pivot, link, side = precisions[0], couplings[0], right_sides[0]
    rows = pivot.shape[0]
    me = lax.axis_index("row")
    places = me ^ jnp.arange(lax.axis_size("row"), dtype=jnp.int32)
    link = jnp.where(lax.axis_index("tm") == 0, jnp.zeros_like(link), link)
    next_rows = from_behind(link, "tm", -1)
    for level in range(LEVELS):
        h = 1 << level
        pieces, link, next_rows = lax.optimization_barrier((gather_pieces(pivot), link, next_rows))
        whole_link = lax.all_gather(link, "row", axis=0, tiled=True)
        next_link = lax.all_gather(next_rows, "row", axis=0, tiled=True)
        whole_side = jnp.zeros((pivot.shape[1], side.shape[1]), side.dtype)
        for k, piece in enumerate(gather_pieces(side)):
            whole_side = lax.dynamic_update_slice(whole_side, piece, (places[k] * rows, 0))
        negative = negative_inverse(places, pieces)
        next_cols = lax.dynamic_slice_in_dim(next_link, me * rows, rows, 1)
        left = multiply(link, negative, ((1,), (0,)))
        right = multiply(next_cols, negative, ((0,), (0,)))
        right_block = multiply(right, next_link, ((1,), (0,)))
        left_block = multiply(left, whole_link, ((1,), (1,)))
        if level + 1 < LEVELS:
            left, right, right_block, left_block = lax.optimization_barrier(
                (left, right, right_block, left_block)
            )
        new_link = multiply(left, next_link, ((1,), (0,)))
        left_side = multiply(left, whole_side, ((1,), (0,)))
        right_side = multiply(right, whole_side, ((1,), (0,)))
        pivot = pivot + from_behind(left_block, "tm", -h) + from_behind(right_block, "tm", h)
        side = side + from_behind(left_side, "tm", -h) + from_behind(right_side, "tm", h)
        link = from_behind(new_link, "tm", h)
        next_rows = from_behind(new_link, "tm", -h)
    return pivot[None], link[None], side[None]


def solution(mesh):
    placed = (P("tm", "row", None), P("tm", "row", None), P("tm", "row", None))
    return jax.shard_map(
        local, mesh=mesh, in_specs=placed, out_specs=placed, check_vma=False
    )
```
